32 devices in a mesh: dom: 8 (over z, y), member: 4 (over x, core).
Axes of the slice: x: 2, y: 2, z: 4, core: 2. Of those that a mesh axis runs over, the one named last changes fastest.
Arguments:
- state: float32 [32, 768, 512], P('member', 'dom'), may hold values from -6 to 6
- noise: bfloat16 [8, 32, 768, 512], P(None, 'member', 'dom'), may hold values from -1.75 to 1.75
- w_local: bfloat16 [512, 512], replicated, may hold values from -0.25 to 0.25
- conn_weight: float32 [16, 768], P(None, 'dom'), may hold values from -1.75 to 1.75
- conn_index: int32 [16, 768], P(None, 'dom'), may hold values from 0 to 127, as said below
- boundary: int32 [8, 8], P('dom'), may hold values from 0 to 95, as said below
- send_pos: int32 [8, 8, 4], replicated, may hold values from 0 to 7
- readout: float32 [512], replicated, may hold values from -0.25 to 0.25
- observed: int32 [8, 64], P('dom'), may hold values from 0 to 95, as said below
- obs_value: float32 [8, 64], P('dom'), may hold values from -6 to 6
- obs_var: float32 [8, 64], P('dom'), may hold values from 0.1 to 1
- obs_pert: float32 [32, 8, 64], P('member', 'dom'), may hold values from -6 to 6
Outputs:
- analysis: float32 [32, 768, 512], P('member', 'dom')
The draws below stay inside these ranges and needn't reach their ends.
Inputs may be any that keep to these rules, and one draw needn't show every extreme that they name: `conn_index`: each voxel's inputs number 12 rows of its own part (below 96) and 4 received slots; every slot is read by some voxel of its part. Each part's boundary rows are distinct. Each part's observed rows are distinct.
All inputs are finite; a program needn't handle non-finite values.
Results may differ from the reference program's by a relative error of at most 0.025.
Values may be sent and summed in bfloat16 or wider, within the bound.
A program may use at most 64 MiB of HBM per device.

```python
import math
import jax
import jax.numpy as jnp
from jax import lax

STATE = 512
VOX_DEV = 96
STEPS = 8
CAP = 4
BND = 8
OBS = 64
KL = 12
KH = 4
KIN = 16
HALO = 32
VOXELS = 768
MEMBERS = 32
N_DOM = 8


def part_perms(key, length):
    keys = jax.random.split(key, N_DOM)
    return jax.vmap(lambda single: jax.random.permutation(single, length))(keys).astype(jnp.int32)


def draw_conn_index(key, part):
    local_rows = jax.random.randint(jax.random.fold_in(key, 11), (KL, VOXELS), 0, VOX_DEV).astype(jnp.int32)
    perms = part_perms(jax.random.fold_in(key, 12), HALO)
    position = (jnp.arange(VOX_DEV, dtype=jnp.int32)[None, :] * KH + jnp.arange(KH, dtype=jnp.int32)[:, None]) % HALO
    halo_rows = perms[:, position]
    halo_rows = jnp.transpose(halo_rows, (1, 0, 2)).reshape(KH, VOXELS) + VOX_DEV
    return jnp.concatenate([local_rows, halo_rows.astype(jnp.int32)], axis=0)


def draw_boundary(key, part):
    return part_perms(jax.random.fold_in(key, 21), VOX_DEV)[:, :BND]


def draw_observed(key, part):
    return part_perms(jax.random.fold_in(key, 31), VOX_DEV)[:, :OBS]


def place_ends(result, own_key, low, largest):
    extent = result.shape
    place = [jax.random.randint(jax.random.fold_in(own_key, axis), (), 0, extent[axis]) for axis in range(len(extent))]
    result = result.at[tuple(place)].set(low)
    longest = extent.index(max(extent))
    place[longest] = (place[longest] + 1) % extent[longest]
    return result.at[tuple(place)].set(largest)


def shard_levels(key, extent, cuts, least, high):
    level = 1.0
    for dim, blocks in cuts:
        steps = jax.random.uniform(jax.random.fold_in(jax.random.fold_in(key, 6), dim), (blocks,), jnp.float32, least / len(cuts), high / len(cuts))
        level = level * jnp.repeat(jnp.exp(steps), extent[dim] // blocks).reshape((-1,) + (1,) * (len(extent) - 1 - dim))
    return level


def centred(key, extent, width, limit, cuts=(), kind=jnp.bfloat16):
    values = jax.random.normal(key, extent, jnp.float32) * width
    if len(cuts) > 0:
        values = shard_levels(key, extent, cuts, -0.22, 0.18) * values
    return jnp.clip(values, min=-limit, max=limit).astype(kind)


def setup_inputs(seed: int = 0) -> dict:
    seeds = jax.random.split(jax.random.key(seed), 13)
    state = centred(seeds[0], (MEMBERS, VOXELS, STATE), 1.0, 6.0, ((0, 4), (1, 8)), jnp.float32)
    noise = centred(seeds[1], (STEPS, MEMBERS, VOXELS, STATE), 0.3, 1.75, ((1, 4), (2, 8)))
    w_local = centred(seeds[2], (STATE, STATE), STATE ** -0.5, 0.25)
    conn_weight = centred(seeds[3], (KIN, VOXELS), 0.3, 1.75, ((1, 8),), jnp.float32)
    conn_index = draw_conn_index(jax.random.fold_in(seeds[12], 71), 0)
    boundary = draw_boundary(jax.random.fold_in(seeds[12], 71), 0)
    send_pos = place_ends(jax.random.randint(seeds[6], (N_DOM, N_DOM, CAP), 0, BND), jax.random.fold_in(seeds[6], 1), 0, BND - 1).astype(jnp.int32)
    readout = centred(seeds[7], (STATE,), 0.044, 0.25, (), jnp.float32)
    observed = draw_observed(jax.random.fold_in(seeds[12], 71), 0)
    obs_value = centred(seeds[9], (N_DOM, OBS), 1.0, 6.0, ((0, 8),), jnp.float32)
    obs_var = jnp.clip(jnp.exp(math.log(1.0) - 2.3025851 * jax.random.uniform(seeds[10], (N_DOM, OBS), jnp.float32) ** shard_levels(seeds[10], (N_DOM, OBS), ((0, 8),), -0.2, 0.2)), 0.1, 1.0)
    obs_pert = centred(seeds[11], (MEMBERS, N_DOM, OBS), 1.0, 6.0, ((0, 4), (1, 8)), jnp.float32)
    return dict(state=state, noise=noise, w_local=w_local, conn_weight=conn_weight, conn_index=conn_index, boundary=boundary, send_pos=send_pos, readout=readout, observed=observed, obs_value=obs_value, obs_var=obs_var, obs_pert=obs_pert)


RELAX_RATE = 0.5

def mixing_matrix(image_part, innov_part, var_part):
    members_count = image_part.shape[0]
    anomaly = image_part - lax.optimization_barrier(jnp.mean(image_part, axis=0, keepdims=True))
    covar = jnp.dot(anomaly.T, anomaly, precision=lax.Precision.HIGHEST) / (members_count - 1) + jnp.diag(var_part)
    gain = jnp.linalg.solve(covar, innov_part.T).T
    mixing = jnp.dot(gain, anomaly.T, precision=lax.Precision.HIGHEST) / (members_count - 1)
    return mixing - lax.optimization_barrier(jnp.mean(mixing, axis=1, keepdims=True))

def reference(state, noise, w_local, conn_weight, conn_index, boundary, send_pos, readout, observed, obs_value, obs_var, obs_pert):
    parts = jnp.arange(N_DOM, dtype=jnp.int32)
    flipped = jnp.transpose(send_pos, (1, 0, 2))
    slot_rows = parts[None, :, None] * VOX_DEV + boundary[parts[None, :, None], flipped]
    slot_rows = slot_rows.reshape(N_DOM, HALO).astype(jnp.int32)
    part_of = jnp.arange(VOXELS, dtype=jnp.int32) // VOX_DEV
    halo_pos = jnp.clip(conn_index - VOX_DEV, 0, HALO - 1)
    global_index = jnp.where(conn_index < VOX_DEV, part_of[None, :] * VOX_DEV + conn_index, slot_rows[part_of[None, :], halo_pos]).astype(jnp.int32)
    current = state
    for step_index in range(STEPS):
        rate = jnp.tanh(current).astype(jnp.bfloat16)

        def add_input(which, total):
            picked = jnp.take(rate, global_index[which], axis=1).astype(jnp.float32)
            return total + conn_weight[which][None, :, None] * picked
        drive = lax.fori_loop(0, KIN, add_input, jnp.zeros(current.shape, jnp.float32))
        inputs = (rate.astype(jnp.float32) + drive).astype(jnp.bfloat16)
        mixed = jnp.dot(inputs.reshape(-1, STATE).astype(jnp.float32), w_local.astype(jnp.float32), preferred_element_type=jnp.float32).reshape(current.shape)
        current = (1.0 - RELAX_RATE) * current + RELAX_RATE * mixed + noise[step_index].astype(jnp.float32)
    rows_observed = (parts[:, None] * VOX_DEV + observed).reshape(-1).astype(jnp.int32)
    picked_obs = jnp.take(current, rows_observed, axis=1)
    image = jnp.einsum('mos,s->mo', picked_obs, readout, precision=lax.Precision.HIGHEST).reshape(MEMBERS, N_DOM, OBS)
    innov = obs_value[None] + jnp.sqrt(obs_var)[None] * obs_pert - image
    mixing = jax.vmap(mixing_matrix, in_axes=(1, 1, 0))(image, innov, obs_var)
    blocks = current.reshape(MEMBERS, N_DOM, VOX_DEV * STATE)
    update = jnp.einsum('pmj,jpf->mpf', mixing, blocks, precision=lax.Precision.HIGHEST)
    return (blocks + update).reshape(MEMBERS, VOXELS, STATE)
```

```python
import functools

import jax
import jax.numpy as jnp
from jax import lax
from jax.experimental import pallas as pl
from jax.experimental.pallas import tpu as pltpu
from jax.sharding import PartitionSpec as P

MESH = pl.DeviceIdType.MESH
HIGHEST = lax.Precision.HIGHEST
F32 = jnp.float32
BF16 = jnp.bfloat16


def kernel(
    n,
    nm,
    group,
    cap,
    chunk,
    state_hbm,
    noise_hbm,
    w_ref,
    conn_ref,
    sel_ref,
    readout_ref,
    observed_ref,
    value_ref,
    var_ref,
    pert_ref,
    out_hbm,
    cur,
    noise,
    rate,
    sendbuf,
    recvbuf,
    ens,
    images,
    padded,
    state_sem,
    noise_sem,
    send_sem,
    recv_sem,
    ens_send,
    ens_recv,
    fwd_send,
    img_send,
    img_recv,
    out_sem,
):
    members, vox, width = cur.shape
    steps = noise.shape[0]
    groups = members // group
    block = group * cap
    me = lax.axis_index("dom")
    mi = lax.axis_index("member")
    sib = mi + 1 - 2 * lax.rem(mi, 2)
    chunks = vox // chunk

    def dom_peer(d):
        return lax.rem(me + d, n)

    def mem_peer(d):
        return lax.rem(mi + d, nm)

    def state_copy(g):
        rows = pl.ds(g * group, group)
        return pltpu.make_async_copy(state_hbm.at[rows], cur.at[rows], state_sem.at[g])

    def noise_copy(k):
        return pltpu.make_async_copy(noise_hbm.at[k], noise.at[k], noise_sem.at[k])

    for g in range(groups):
        state_copy(g).start()
    for k in range(steps):
        noise_copy(k).start()

    barrier = pltpu.get_barrier_semaphore()
    for d in range(1, n):
        pl.semaphore_signal(barrier, inc=1, device_id=(dom_peer(d), mi), device_id_type=MESH)
    for d in range(1, nm):
        pl.semaphore_signal(barrier, inc=1, device_id=(me, mem_peer(d)), device_id_type=MESH)

    def halo_copy(g, slot, d):
        return pltpu.make_async_remote_copy(
            src_ref=sendbuf.at[g, slot, dom_peer(d)],
            dst_ref=recvbuf.at[g, slot, me],
            send_sem=send_sem.at[g, slot, d],
            recv_sem=recv_sem.at[g, slot, d],
            device_id=(dom_peer(d), mi),
            device_id_type=MESH,
        )

    def halo_arrival(g, slot, d):
        source = lax.rem(me + n - d, n)
        return pltpu.make_async_remote_copy(
            src_ref=sendbuf.at[g, slot, source],
            dst_ref=recvbuf.at[g, slot, source],
            send_sem=send_sem.at[g, slot, d],
            recv_sem=recv_sem.at[g, slot, d],
            device_id=(source, mi),
            device_id_type=MESH,
        )

    order = sorted(range(1, n), key=lambda d: abs(2 * d - n))

    def make_rate(g):
        rows = pl.ds(g * group, group)
        rate[rows] = jnp.tanh(cur[rows]).astype(BF16)

    def send(g, slot):
        rows = pl.ds(g * group, group)
        picked = jnp.dot(
            sel_ref[...], rate[rows].reshape(group * vox, width), preferred_element_type=F32
        )
        sendbuf[g, slot] = picked.astype(BF16).reshape(n, block, width)
        for d in order:
            halo_copy(g, slot, d).start()
        recvbuf[g, slot, me] = sendbuf[g, slot, me]

    def receive(g, slot):
        for d in order:
            halo_arrival(g, slot, d).wait_recv()
        for d in order:
            halo_copy(g, slot, d).wait_send()

    def update(g, slot, k):
        halo = recvbuf[g, slot].reshape(n * block, width)
        for m in range(group):
            i = g * group + m
            table = jnp.concatenate([halo, rate[i]], axis=0)
            inputs = jnp.dot(conn_ref[m], table, preferred_element_type=F32).astype(BF16)
            mixed = jnp.dot(inputs, w_ref[...], preferred_element_type=F32)
            cur[i] = 0.5 * (cur[i] + mixed) + noise[k, i].astype(F32)

    for g in range(groups):
        state_copy(g).wait()
        make_rate(g)
        if g == 0:
            pl.semaphore_wait(barrier, n - 1 + nm - 1)
        send(g, 0)

    def step(k, carry):
        slot = lax.rem(k, 2)
        noise_copy(k).wait()
        for g in range(groups):
            receive(g, slot)
            update(g, slot, k)
            make_rate(g)
            send(g, 1 - slot)
        return carry

    lax.fori_loop(0, steps - 1, step, 0)

    def ens_piece(dev, g, c):
        return ens.at[dev, g, :, pl.ds(c * chunk, chunk)]

    def ens_copy(dev, g, c, target, send_to, recv_to):
        return pltpu.make_async_remote_copy(
            src_ref=ens_piece(dev, g, c),
            dst_ref=ens_piece(dev, g, c),
            send_sem=send_to,
            recv_sem=recv_to,
            device_id=(me, target),
            device_id_type=MESH,
        )

    far = range(2, nm, 2)

    def own_copy(g, c, d):
        target = sib if d == 0 else mem_peer(d)
        return ens_copy(mi, g, c, target, ens_send.at[g, c, d // 2], ens_recv.at[g, c, d // 2])

    def own_arrival(g, c, d):
        source = sib if d == 0 else lax.rem(mi + nm - d, nm)
        return ens_copy(source, g, c, source, ens_send.at[g, c, d // 2], ens_recv.at[g, c, d // 2])

    def forward_copy(g, c, d):
        source = lax.rem(mi + nm - d, nm)
        return ens_copy(
            source, g, c, sib, fwd_send.at[g, c, d // 2], ens_recv.at[g, c, nm // 2 + d // 2]
        )

    def forward_arrival(g, c, d):
        source = lax.rem(sib + nm - d, nm)
        return ens_copy(
            source, g, c, sib, fwd_send.at[g, c, d // 2], ens_recv.at[g, c, nm // 2 + d // 2]
        )

    obs = observed_ref.shape[1]
    padded[...] = jnp.zeros_like(padded)
    padded[0:1, 0:obs] = value_ref[...]
    padded[1:2, :] = jnp.ones((1, padded.shape[1]), F32)
    padded[1:2, 0:obs] = var_ref[...]
    padded[2:3, 0:obs] = observed_ref[...].astype(F32) + 1.0
    padded[8 : 8 + members, 0:obs] = pert_ref[:, 0, :]
    lanes = padded.shape[1]
    vox_iota = lax.broadcasted_iota(jnp.int32, (vox, lanes), 0).astype(F32) + 1.0
    pick = jnp.where(vox_iota == padded[2:3, :], 1.0, 0.0)

    last = steps - 1
    slot = last % 2
    noise_copy(last).wait()
    for g in range(groups):
        receive(g, slot)
        update(g, slot, last)
        rows = pl.ds(g * group, group)
        ens[mi, g] = cur[rows].astype(BF16)
        for c in range(chunks):
            for d in far:
                own_copy(g, c, d).start()
        for c in range(chunks):
            own_copy(g, c, 0).start()
        for m in range(group):
            seen = jnp.sum(cur[g * group + m] * readout_ref[...], axis=1, keepdims=True)
            images[mi, g * group + m, :] = jnp.sum(pick * seen, axis=0)

    def img_copy(d):
        return pltpu.make_async_remote_copy(
            src_ref=images.at[mi],
            dst_ref=images.at[mi],
            send_sem=img_send.at[d],
            recv_sem=img_recv.at[d],
            device_id=(me, mem_peer(d)),
            device_id_type=MESH,
        )

    def img_arrival(d):
        source = lax.rem(mi + nm - d, nm)
        return pltpu.make_async_remote_copy(
            src_ref=images.at[source],
            dst_ref=images.at[source],
            send_sem=img_send.at[d],
            recv_sem=img_recv.at[d],
            device_id=(me, source),
            device_id_type=MESH,
        )

    for d in range(1, nm):
        img_copy(d).start()
    for d in range(1, nm):
        img_arrival(d).wait_recv()

    total = nm * members
    var = padded[1:2, :]
    innov = padded[0:1, :] + jnp.sqrt(var) * padded[8 : 8 + members, :] - images[mi]
    image_all = images[...].reshape(total, lanes)
    anomaly = image_all - jnp.mean(image_all, axis=0, keepdims=True)
    scaled = anomaly / (var * (total - 1))
    nt = (((1,), (1,)), ((), ()))
    system = lax.dot_general(
        scaled,
        jnp.concatenate([anomaly, innov], axis=0),
        nt,
        precision=HIGHEST,
        preferred_element_type=F32,
    )
    row_id = lax.broadcasted_iota(jnp.int32, system.shape, 0)
    col_id = lax.broadcasted_iota(jnp.int32, system.shape, 1)
    system = system + jnp.where(row_id == col_id, 1.0, 0.0)
    column_rows = lax.broadcasted_iota(jnp.int32, (total, 1), 0)
    for j in range(total):
        row = system[j : j + 1, :] / system[j : j + 1, j : j + 1]
        column = system[:, j : j + 1] - jnp.where(column_rows == j, 1.0, 0.0)
        system = system - column * row
    mix = system[:, total : total + members]
    mix = mix - jnp.mean(mix, axis=0, keepdims=True)

    sub = 16
    e1 = jnp.where(
        lax.broadcasted_iota(jnp.int32, (members * sub, members), 0) // sub
        == lax.broadcasted_iota(jnp.int32, (members * sub, members), 1),
        1.0,
        0.0,
    )
    e2 = jnp.where(
        lax.broadcasted_iota(jnp.int32, (total, total * sub), 1) // sub
        == lax.broadcasted_iota(jnp.int32, (total, total * sub), 0),
        1.0,
        0.0,
    )
    wide = lax.dot_general(e1, mix, nt, precision=HIGHEST, preferred_element_type=F32)
    wide = jnp.dot(wide, e2, precision=HIGHEST, preferred_element_type=F32)
    same = lax.rem(lax.broadcasted_iota(jnp.int32, wide.shape, 0), sub) == lax.rem(
        lax.broadcasted_iota(jnp.int32, wide.shape, 1), sub
    )
    wide = jnp.where(same, wide, 0.0)
    high = wide.astype(BF16)
    low = (wide - high.astype(F32)).astype(BF16)
    both = jnp.concatenate([high, low], axis=0)

    for g in range(groups - 1):
        for c in range(chunks):
            for d in far:
                own_arrival(g, c, d).wait_recv()
                forward_copy(g, c, d).start()
    for c in range(chunks):
        g = groups - 1
        for d in far:
            own_arrival(g, c, d).wait_recv()
            forward_copy(g, c, d).start()
        for g in range(groups):
            own_arrival(g, c, 0).wait_recv()
            for d in far:
                forward_arrival(g, c, d).wait_recv()
        for s in range(chunk // sub):
            rows = pl.ds(c * chunk + s * sub, sub)
            data = ens[:, :, :, rows].reshape(total * sub, width)
            added = jnp.dot(both, data, preferred_element_type=F32)
            half = members * sub
            added = (added[:half] + added[half:]).reshape(members, sub, width)
            cur[:, rows] = cur[:, rows] + added
        piece = pl.ds(c * chunk, chunk)
        pltpu.make_async_copy(cur.at[:, piece], out_hbm.at[:, piece], out_sem.at[c]).start()

    for c in range(chunks):
        piece = pl.ds(c * chunk, chunk)
        pltpu.make_async_copy(cur.at[:, piece], out_hbm.at[:, piece], out_sem.at[c]).wait()
        for g in range(groups):
            own_copy(g, c, 0).wait_send()
            for d in far:
                own_copy(g, c, d).wait_send()
                forward_copy(g, c, d).wait_send()
    for d in range(1, nm):
        img_copy(d).wait_send()


def per_device(
    state,
    noise,
    w_local,
    conn_weight,
    conn_index,
    boundary,
    send_pos,
    readout,
    observed,
    obs_value,
    obs_var,
    obs_pert,
):
    members, vox, width = state.shape
    steps = noise.shape[0]
    n = lax.axis_size("dom")
    nm = lax.axis_size("member")
    me = lax.axis_index("dom")
    cap = send_pos.shape[2]
    obs = observed.shape[1]
    group = max(1, min(members, 16 // cap))
    groups = members // group
    block = group * cap
    chunk = 32

    halo = conn_index - vox
    slots = (halo // cap) * block + lax.rem(halo, cap)
    column = jnp.arange(n * block + vox, dtype=jnp.int32)
    member = jnp.arange(group, dtype=jnp.int32)
    target = jnp.where(
        (halo < 0)[:, None, :],
        (conn_index + n * block)[:, None, :],
        slots[:, None, :] + member[None, :, None] * cap,
    )
    conn = jnp.sum(
        jnp.where(target[..., None] == column, conn_weight[:, None, :, None], 0.0), axis=0
    )
    own = (column[None, :] - n * block) == jnp.arange(vox, dtype=jnp.int32)[:, None]
    conn = (conn + own[None].astype(F32)).astype(BF16)

    mine = lax.dynamic_index_in_dim(send_pos, me, 0, keepdims=False)
    which = jnp.arange(boundary.shape[1], dtype=jnp.int32)
    local = jnp.sum(jnp.where(mine[..., None] == which, boundary[0], 0), axis=-1)
    flat = jnp.arange(group * vox, dtype=jnp.int32)
    sel = flat == local[:, None, :, None] + member[None, :, None, None] * vox
    sel = sel.astype(BF16).reshape(n * block, group * vox)

    vmem = pl.BlockSpec(memory_space=pltpu.VMEM)
    anywhere = pl.BlockSpec(memory_space=pl.ANY)
    dma = pltpu.SemaphoreType.DMA
    chunks = vox // chunk
    lanes = -(-obs // 128) * 128
    return pl.pallas_call(
        functools.partial(kernel, n, nm, group, cap, chunk),
        out_shape=jax.ShapeDtypeStruct(state.shape, F32),
        in_specs=[anywhere, anywhere] + [vmem] * 8,
        out_specs=anywhere,
        scratch_shapes=[
            pltpu.VMEM((members, vox, width), F32),
            pltpu.VMEM((steps, members, vox, width), BF16),
            pltpu.VMEM((members, vox, width), BF16),
            pltpu.VMEM((groups, 2, n, block, width), BF16),
            pltpu.VMEM((groups, 2, n, block, width), BF16),
            pltpu.VMEM((nm, groups, group, vox, width), BF16),
            pltpu.VMEM((nm, members, lanes), F32),
            pltpu.VMEM((8 + members, lanes), F32),
            dma((groups,)),
            dma((steps,)),
            dma((groups, 2, n)),
            dma((groups, 2, n)),
            dma((groups, chunks, nm)),
            dma((groups, chunks, nm)),
            dma((groups, chunks, nm)),
            dma((nm,)),
            dma((nm,)),
            dma((chunks,)),
        ],
        compiler_params=pltpu.CompilerParams(
            collective_id=0, has_side_effects=True, vmem_limit_bytes=48 * 1024 * 1024
        ),
    )(
        state,
        noise,
        w_local,
        conn,
        sel,
        readout[None, :],
        observed,
        obs_value,
        obs_var,
        obs_pert,
    )


def solution(mesh):
    in_specs = (
        P("member", "dom", None),
        P(None, "member", "dom", None),
        P(),
        P(None, "dom"),
        P(None, "dom"),
        P("dom", None),
        P(),
        P(),
        P("dom", None),
        P("dom", None),
        P("dom", None),
        P("member", "dom", None),
    )
    return jax.shard_map(
        per_device,
        mesh=mesh,
        in_specs=in_specs,
        out_specs=P("member", "dom", None),
        check_vma=False,
    )
```

```python
import functools

import jax
import jax.numpy as jnp
from jax import lax
from jax.experimental import pallas as pl
from jax.experimental.pallas import tpu as pltpu
from jax.sharding import PartitionSpec as P

MESH = pl.DeviceIdType.MESH
HIGHEST = lax.Precision.HIGHEST
F32 = jnp.float32
BF16 = jnp.bfloat16


def kernel(
    n,
    nm,
    group,
    cap,
    chunk,
    parts,
    state_hbm,
    noise_hbm,
    w_hbm,
    weight_hbm,
    index_hbm,
    boundary_hbm,
    send_hbm,
    readout_hbm,
    observed_hbm,
    value_hbm,
    var_hbm,
    pert_hbm,
    out_hbm,
    w_ref,
    weight_ref,
    index_ref,
    boundary_ref,
    send_ref,
    readout_ref,
    observed_ref,
    value_ref,
    var_ref,
    pert_ref,
    weight_pad,
    index_pad,
    conn_ref,
    sel_ref,
    small_sem,
    cur,
    noise,
    rate,
    sendbuf,
    recvbuf,
    ens,
    images,
    padded,
    state_sem,
    noise_sem,
    send_sem,
    recv_sem,
    ens_send,
    ens_recv,
    fwd_send,
    img_send,
    img_recv,
    out_sem,
):
    members, vox, width = cur.shape
    steps = noise.shape[0]
    groups = members // group
    pseudo = group * parts
    part = width // parts
    block = pseudo * cap
    me = lax.axis_index("dom")
    mi = lax.axis_index("member")
    sib = mi + 1 - 2 * lax.rem(mi, 2)
    chunks = vox // chunk

    def dom_peer(d):
        return lax.rem(me + d, n)

    def mem_peer(d):
        return lax.rem(mi + d, nm)

    def state_copy(g):
        rows = pl.ds(g * group, group)
        return pltpu.make_async_copy(state_hbm.at[rows], cur.at[rows], state_sem.at[g])

    def noise_copy(k):
        return pltpu.make_async_copy(noise_hbm.at[k], noise.at[k], noise_sem.at[k])

    small = [
        pltpu.make_async_copy(a, b, small_sem.at[i])
        for i, (a, b) in enumerate(
            (
                (weight_hbm, weight_ref),
                (index_hbm, index_ref),
                (boundary_hbm, boundary_ref),
                (send_hbm, send_ref),
                (w_hbm, w_ref),
                (readout_hbm, readout_ref),
                (observed_hbm, observed_ref),
                (value_hbm, value_ref),
                (var_hbm, var_ref),
                (pert_hbm, pert_ref),
            )
        )
    ]
    for copy in small[:4]:
        copy.start()
    state_copy(0).start()
    for copy in small[4:]:
        copy.start()
    for g in range(1, groups):
        state_copy(g).start()
    for k in range(steps):
        noise_copy(k).start()

    barrier = pltpu.get_barrier_semaphore()
    for d in range(1, n):
        pl.semaphore_signal(barrier, inc=1, device_id=(dom_peer(d), mi), device_id_type=MESH)
    for d in range(1, nm):
        pl.semaphore_signal(barrier, inc=1, device_id=(me, mem_peer(d)), device_id_type=MESH)

    def halo_copy(g, slot, d):
        return pltpu.make_async_remote_copy(
            src_ref=sendbuf.at[g, slot, dom_peer(d)],
            dst_ref=recvbuf.at[g, slot, me],
            send_sem=send_sem.at[g, slot, d],
            recv_sem=recv_sem.at[g, slot, d],
            device_id=(dom_peer(d), mi),
            device_id_type=MESH,
        )

    def halo_arrival(g, slot, d):
        source = lax.rem(me + n - d, n)
        return pltpu.make_async_remote_copy(
            src_ref=sendbuf.at[g, slot, source],
            dst_ref=recvbuf.at[g, slot, source],
            send_sem=send_sem.at[g, slot, d],
            recv_sem=recv_sem.at[g, slot, d],
            device_id=(source, mi),
            device_id_type=MESH,
        )

    order = sorted(range(1, n), key=lambda d: abs(2 * d - n))

    for copy in small:
        copy.wait()

    wide_vox = weight_pad.shape[1]
    halo_rows = n * block
    index_pad[...] = jnp.full_like(index_pad, -1)
    weight_pad[...] = jnp.zeros_like(weight_pad)
    index_pad[:, 0:vox] = index_ref[...]
    weight_pad[:, 0:vox] = weight_ref[...]
    index = index_pad[...]
    weight = weight_pad[...]
    beyond = index - vox
    slots = jnp.where(beyond < 0, -1 - halo_rows, (beyond // cap) * block + beyond % cap)
    halo_iota = lax.broadcasted_iota(jnp.int32, (halo_rows, wide_vox), 0)
    own_iota = lax.broadcasted_iota(jnp.int32, (wide_vox, wide_vox), 0)
    own_lane = lax.broadcasted_iota(jnp.int32, (wide_vox, wide_vox), 1)
    own = jnp.where(own_iota == own_lane, 1.0, 0.0)
    for k in range(index.shape[0]):
        own = own + jnp.where(own_iota == index[k : k + 1], weight[k : k + 1], 0.0)
    own = own.T[:vox, :vox].astype(BF16)
    for m in range(pseudo):
        matrix = jnp.zeros((halo_rows, wide_vox), F32)
        for k in range(index.shape[0]):
            target = slots[k : k + 1] + m * cap
            matrix = matrix + jnp.where(halo_iota == target, weight[k : k + 1], 0.0)
        conn_ref[m, :, 0:halo_rows] = matrix.T[:vox].astype(BF16)
        conn_ref[m, :, halo_rows : halo_rows + vox] = own

    mine = send_ref[me]
    local = jnp.zeros((n, cap), jnp.int32)
    for b in range(boundary_ref.shape[1]):
        local = local + jnp.where(mine == b, boundary_ref[0:1, b : b + 1], 0)
    spread = jnp.where(
        lax.broadcasted_iota(jnp.int32, (cap, halo_rows), 1) % cap
        == lax.broadcasted_iota(jnp.int32, (cap, halo_rows), 0),
        1.0,
        0.0,
    )
    spread = jnp.dot(
        local.astype(F32), spread, precision=HIGHEST, preferred_element_type=F32
    )
    mine_row = lax.broadcasted_iota(jnp.int32, (n, halo_rows), 1) // block
    spread = jnp.where(
        mine_row == lax.broadcasted_iota(jnp.int32, (n, halo_rows), 0), spread, 0.0
    )
    source_row = jnp.sum(spread, axis=0, keepdims=True)
    lane = lax.broadcasted_iota(jnp.int32, (wide_vox, halo_rows), 1)
    lane_member = (lane % block) // cap
    voxel = lax.broadcasted_iota(jnp.int32, (wide_vox, halo_rows), 0).astype(F32)
    chosen = jnp.where(voxel == source_row, 1.0, 0.0)
    for m in range(pseudo):
        matrix = jnp.where(lane_member == m, chosen, 0.0)
        sel_ref[:, m * vox : (m + 1) * vox] = matrix.T[:, :vox].astype(BF16)

    def make_rate(g):
        rows = pl.ds(g * group, group)
        rate[rows] = jnp.tanh(cur[rows]).astype(BF16)

    def pieces(g):
        for h in range(parts):
            for m in range(group):
                yield rate[g * group + m, :, h * part : (h + 1) * part]

    def send(g, slot):
        picked = jnp.dot(
            sel_ref[...], jnp.concatenate(list(pieces(g)), axis=0), preferred_element_type=F32
        )
        sendbuf[g, slot] = picked.astype(BF16).reshape(n, block, part)
        for d in order:
            halo_copy(g, slot, d).start()
        recvbuf[g, slot, me] = sendbuf[g, slot, me]

    def receive(g, slot):
        for d in order:
            halo_arrival(g, slot, d).wait_recv()
        for d in order:
            halo_copy(g, slot, d).wait_send()

    def update(g, slot, k):
        halo = recvbuf[g, slot].reshape(halo_rows, part)
        drives = [
            jnp.dot(
                conn_ref[i],
                jnp.concatenate([halo, own_rows], axis=0),
                preferred_element_type=F32,
            ).astype(BF16)
            for i, own_rows in enumerate(pieces(g))
        ]
        inputs = jnp.concatenate(
            [
                jnp.concatenate([drives[h * group + m] for h in range(parts)], axis=1)
                for m in range(group)
            ],
            axis=0,
        )
        mixed = jnp.dot(inputs, w_ref[...], preferred_element_type=F32)
        rows = pl.ds(g * group, group)
        mixed = mixed.reshape(group, vox, width)
        cur[rows] = 0.5 * (cur[rows] + mixed) + noise[k, rows].astype(F32)

    def ens_piece(dev, g, c):
        return ens.at[dev, g, :, pl.ds(c * chunk, chunk)]

    def ens_copy(dev, g, c, target, send_to, recv_to):
        return pltpu.make_async_remote_copy(
            src_ref=ens_piece(dev, g, c),
            dst_ref=ens_piece(dev, g, c),
            send_sem=send_to,
            recv_sem=recv_to,
            device_id=(me, target),
            device_id_type=MESH,
        )

    far = range(2, nm, 2)

    def own_copy(g, c, d):
        target = sib if d == 0 else mem_peer(d)
        return ens_copy(mi, g, c, target, ens_send.at[g, c, d // 2], ens_recv.at[g, c, d // 2])

    def own_arrival(g, c, d):
        source = sib if d == 0 else lax.rem(mi + nm - d, nm)
        return ens_copy(source, g, c, source, ens_send.at[g, c, d // 2], ens_recv.at[g, c, d // 2])

    def forward_copy(g, c, d):
        source = lax.rem(mi + nm - d, nm)
        return ens_copy(
            source, g, c, sib, fwd_send.at[g, c, d // 2], ens_recv.at[g, c, nm // 2 + d // 2]
        )

    def forward_arrival(g, c, d):
        source = lax.rem(sib + nm - d, nm)
        return ens_copy(
            source, g, c, sib, fwd_send.at[g, c, d // 2], ens_recv.at[g, c, nm // 2 + d // 2]
        )

    obs = observed_ref.shape[1]
    padded[...] = jnp.zeros_like(padded)
    padded[0:1, 0:obs] = value_ref[...]
    padded[1:2, :] = jnp.ones((1, padded.shape[1]), F32)
    padded[1:2, 0:obs] = var_ref[...]
    padded[2:3, 0:obs] = observed_ref[...].astype(F32) + 1.0
    padded[8 : 8 + members, 0:obs] = pert_ref[:, 0, :]
    lanes = padded.shape[1]
    vox_iota = lax.broadcasted_iota(jnp.int32, (vox, lanes), 0).astype(F32) + 1.0
    pick = jnp.where(vox_iota == padded[2:3, :], 1.0, 0.0)

    def finish(g):
        rows = pl.ds(g * group, group)
        ens[mi, g] = cur[rows].astype(BF16)
        for c in range(chunks):
            for d in far:
                own_copy(g, c, d).start()
        for c in range(chunks):
            own_copy(g, c, 0).start()
        for m in range(group):
            seen = jnp.sum(cur[g * group + m] * readout_ref[...], axis=1, keepdims=True)
            images[mi, g * group + m, :] = jnp.sum(pick * seen, axis=0)

    last = steps - 1
    flight = 2 if groups % 2 == 0 else 1
    for g in range(flight):
        state_copy(g).wait()
        make_rate(g)
        if g == 0:
            pl.semaphore_wait(barrier, n - 1 + nm - 1)
        send(g, 0)
    for k in range(steps):
        noise_copy(k).wait()
    for first in range(0, groups, flight):

        def step(k, carry):
            slot = lax.rem(k, 2)
            for g in range(first, first + flight):
                receive(g, slot)
                update(g, slot, k)
                make_rate(g)
                send(g, 1 - slot)
            return carry

        lax.fori_loop(0, last, step, 0)
        for g in range(first, first + flight):
            receive(g, last % 2)
            update(g, last % 2, last)
            if g + flight < groups:
                state_copy(g + flight).wait()
                make_rate(g + flight)
                send(g + flight, 0)
            finish(g)

    def img_copy(d):
        return pltpu.make_async_remote_copy(
            src_ref=images.at[mi],
            dst_ref=images.at[mi],
            send_sem=img_send.at[d],
            recv_sem=img_recv.at[d],
            device_id=(me, mem_peer(d)),
            device_id_type=MESH,
        )

    def img_arrival(d):
        source = lax.rem(mi + nm - d, nm)
        return pltpu.make_async_remote_copy(
            src_ref=images.at[source],
            dst_ref=images.at[source],
            send_sem=img_send.at[d],
            recv_sem=img_recv.at[d],
            device_id=(me, source),
            device_id_type=MESH,
        )

    for d in range(1, nm):
        img_copy(d).start()
    for d in range(1, nm):
        img_arrival(d).wait_recv()

    total = nm * members
    var = padded[1:2, :]
    innov = padded[0:1, :] + jnp.sqrt(var) * padded[8 : 8 + members, :] - images[mi]
    image_all = images[...].reshape(total, lanes)
    anomaly = image_all - jnp.mean(image_all, axis=0, keepdims=True)
    scaled = anomaly / (var * (total - 1))
    nt = (((1,), (1,)), ((), ()))
    system = lax.dot_general(
        scaled,
        jnp.concatenate([anomaly, innov], axis=0),
        nt,
        precision=HIGHEST,
        preferred_element_type=F32,
    )
    row_id = lax.broadcasted_iota(jnp.int32, system.shape, 0)
    col_id = lax.broadcasted_iota(jnp.int32, system.shape, 1)
    system = system + jnp.where(row_id == col_id, 1.0, 0.0)
    column_rows = lax.broadcasted_iota(jnp.int32, (total, 1), 0)
    for j in range(total):
        row = system[j : j + 1, :] / system[j : j + 1, j : j + 1]
        column = system[:, j : j + 1] - jnp.where(column_rows == j, 1.0, 0.0)
        system = system - column * row
    mix = system[:, total : total + members]
    mix = mix - jnp.mean(mix, axis=0, keepdims=True)

    sub = 16
    e1 = jnp.where(
        lax.broadcasted_iota(jnp.int32, (members * sub, members), 0) // sub
        == lax.broadcasted_iota(jnp.int32, (members * sub, members), 1),
        1.0,
        0.0,
    )
    e2 = jnp.where(
        lax.broadcasted_iota(jnp.int32, (total, total * sub), 1) // sub
        == lax.broadcasted_iota(jnp.int32, (total, total * sub), 0),
        1.0,
        0.0,
    )
    wide = lax.dot_general(e1, mix, nt, precision=HIGHEST, preferred_element_type=F32)
    wide = jnp.dot(wide, e2, precision=HIGHEST, preferred_element_type=F32)
    same = lax.rem(lax.broadcasted_iota(jnp.int32, wide.shape, 0), sub) == lax.rem(
        lax.broadcasted_iota(jnp.int32, wide.shape, 1), sub
    )
    wide = jnp.where(same, wide, 0.0)
    high = wide.astype(BF16)
    low = (wide - high.astype(F32)).astype(BF16)
    both = jnp.concatenate([high, low], axis=0)

    for g in range(groups - 1):
        for c in range(chunks):
            for d in far:
                own_arrival(g, c, d).wait_recv()
                forward_copy(g, c, d).start()
    for c in range(chunks):
        g = groups - 1
        for d in far:
            own_arrival(g, c, d).wait_recv()
            forward_copy(g, c, d).start()
        for g in range(groups):
            own_arrival(g, c, 0).wait_recv()
            for d in far:
                forward_arrival(g, c, d).wait_recv()
        for s in range(chunk // sub):
            rows = pl.ds(c * chunk + s * sub, sub)
            data = ens[:, :, :, rows].reshape(total * sub, width)
            added = jnp.dot(both, data, preferred_element_type=F32)
            half = members * sub
            added = (added[:half] + added[half:]).reshape(members, sub, width)
            cur[:, rows] = cur[:, rows] + added
        piece = pl.ds(c * chunk, chunk)
        pltpu.make_async_copy(cur.at[:, piece], out_hbm.at[:, piece], out_sem.at[c]).start()

    for c in range(chunks):
        piece = pl.ds(c * chunk, chunk)
        pltpu.make_async_copy(cur.at[:, piece], out_hbm.at[:, piece], out_sem.at[c]).wait()
        for g in range(groups):
            own_copy(g, c, 0).wait_send()
            for d in far:
                own_copy(g, c, d).wait_send()
                forward_copy(g, c, d).wait_send()
    for d in range(1, nm):
        img_copy(d).wait_send()


def per_device(
    state,
    noise,
    w_local,
    conn_weight,
    conn_index,
    boundary,
    send_pos,
    readout,
    observed,
    obs_value,
    obs_var,
    obs_pert,
):
    members, vox, width = state.shape
    steps = noise.shape[0]
    n = lax.axis_size("dom")
    nm = lax.axis_size("member")
    cap = send_pos.shape[2]
    obs = observed.shape[1]
    parts = 2
    group = max(1, 16 // (cap * parts))
    groups = members // group
    block = group * parts * cap
    chunk = 32
    wide_vox = -(-vox // 128) * 128
    halo_rows = n * block

    hbm = pl.BlockSpec(memory_space=pltpu.HBM)
    small = (
        w_local,
        conn_weight,
        conn_index,
        boundary,
        send_pos,
        readout[None, :],
        observed,
        obs_value,
        obs_var,
        obs_pert,
    )
    dma = pltpu.SemaphoreType.DMA
    chunks = vox // chunk
    lanes = -(-obs // 128) * 128
    return pl.pallas_call(
        functools.partial(kernel, n, nm, group, cap, chunk, parts),
        out_shape=jax.ShapeDtypeStruct(state.shape, F32),
        in_specs=[hbm] * 12,
        out_specs=pl.BlockSpec(memory_space=pl.ANY),
        scratch_shapes=[pltpu.VMEM(x.shape, x.dtype) for x in small]
        + [
            pltpu.VMEM((conn_index.shape[0], wide_vox), F32),
            pltpu.VMEM((conn_index.shape[0], wide_vox), jnp.int32),
            pltpu.VMEM((group * parts, vox, halo_rows + vox), BF16),
            pltpu.VMEM((halo_rows, group * parts * vox), BF16),
            dma((len(small),)),
            pltpu.VMEM((members, vox, width), F32),
            pltpu.VMEM((steps, members, vox, width), BF16),
            pltpu.VMEM((members, vox, width), BF16),
            pltpu.VMEM((groups, 2, n, block, width // parts), BF16),
            pltpu.VMEM((groups, 2, n, block, width // parts), BF16),
            pltpu.VMEM((nm, groups, group, vox, width), BF16),
            pltpu.VMEM((nm, members, lanes), F32),
            pltpu.VMEM((8 + members, lanes), F32),
            dma((groups,)),
            dma((steps,)),
            dma((groups, 2, n)),
            dma((groups, 2, n)),
            dma((groups, chunks, nm)),
            dma((groups, chunks, nm)),
            dma((groups, chunks, nm)),
            dma((nm,)),
            dma((nm,)),
            dma((chunks,)),
        ],
        compiler_params=pltpu.CompilerParams(
            collective_id=0, has_side_effects=True, vmem_limit_bytes=62 * 1024 * 1024
        ),
    )(
        state,
        noise,
        *small,
    )


def solution(mesh):
    in_specs = (
        P("member", "dom", None),
        P(None, "member", "dom", None),
        P(),
        P(None, "dom"),
        P(None, "dom"),
        P("dom", None),
        P(),
        P(),
        P("dom", None),
        P("dom", None),
        P("dom", None),
        P("member", "dom", None),
    )
    return jax.shard_map(
        per_device,
        mesh=mesh,
        in_specs=in_specs,
        out_specs=P("member", "dom", None),
        check_vma=False,
    )
```

```python
import functools

import jax
import jax.numpy as jnp
from jax import lax
from jax.experimental import pallas as pl
from jax.experimental.pallas import tpu as pltpu
from jax.sharding import PartitionSpec as P

MESH = pl.DeviceIdType.MESH
HIGHEST = lax.Precision.HIGHEST
F32 = jnp.float32
BF16 = jnp.bfloat16


def kernel(
    n,
    nm,
    group,
    cap,
    chunk,
    parts,
    state_hbm,
    noise_hbm,
    w_hbm,
    weight_hbm,
    index_hbm,
    boundary_hbm,
    send_hbm,
    readout_hbm,
    observed_hbm,
    value_hbm,
    var_hbm,
    pert_hbm,
    out_hbm,
    w_ref,
    weight_ref,
    index_ref,
    boundary_ref,
    send_ref,
    readout_ref,
    observed_ref,
    value_ref,
    var_ref,
    pert_ref,
    weight_pad,
    index_pad,
    conn_ref,
    sel_ref,
    small_sem,
    cur,
    noise,
    rate,
    sendbuf,
    recvbuf,
    ens,
    images,
    padded,
    state_sem,
    noise_sem,
    send_sem,
    recv_sem,
    ens_send,
    ens_recv,
    fwd_send,
    img_send,
    img_recv,
    out_sem,
):
    members, vox, width = cur.shape
    steps = noise.shape[0]
    groups = members // group
    pseudo = group * parts
    part = width // parts
    block = pseudo * cap
    me = lax.axis_index("dom")
    mi = lax.axis_index("member")
    sib = mi + 1 - 2 * lax.rem(mi, 2)
    chunks = vox // chunk

    def dom_peer(d):
        return lax.rem(me + d, n)

    def mem_peer(d):
        return lax.rem(mi + d, nm)

    def state_copy(g):
        rows = pl.ds(g * group, group)
        return pltpu.make_async_copy(state_hbm.at[rows], cur.at[rows], state_sem.at[g])

    def noise_copy(k):
        return pltpu.make_async_copy(noise_hbm.at[k], noise.at[k], noise_sem.at[k])

    small = [
        pltpu.make_async_copy(a, b, small_sem.at[i])
        for i, (a, b) in enumerate(
            (
                (weight_hbm, weight_ref),
                (index_hbm, index_ref),
                (boundary_hbm, boundary_ref),
                (send_hbm, send_ref),
                (w_hbm, w_ref),
                (readout_hbm, readout_ref),
                (observed_hbm, observed_ref),
                (value_hbm, value_ref),
                (var_hbm, var_ref),
                (pert_hbm, pert_ref),
            )
        )
    ]
    for copy in small[:4]:
        copy.start()
    state_copy(0).start()
    for copy in small[4:]:
        copy.start()
    for g in range(1, groups):
        state_copy(g).start()
    for k in range(steps):
        noise_copy(k).start()

    barrier = pltpu.get_barrier_semaphore()
    for d in range(1, n):
        pl.semaphore_signal(barrier, inc=1, device_id=(dom_peer(d), mi), device_id_type=MESH)
    for d in range(1, nm):
        pl.semaphore_signal(barrier, inc=1, device_id=(me, mem_peer(d)), device_id_type=MESH)

    def halo_copy(g, slot, d):
        return pltpu.make_async_remote_copy(
            src_ref=sendbuf.at[g, slot, dom_peer(d)],
            dst_ref=recvbuf.at[g, slot, me],
            send_sem=send_sem.at[g, slot, d],
            recv_sem=recv_sem.at[g, slot, d],
            device_id=(dom_peer(d), mi),
            device_id_type=MESH,
        )

    def halo_arrival(g, slot, d):
        source = lax.rem(me + n - d, n)
        return pltpu.make_async_remote_copy(
            src_ref=sendbuf.at[g, slot, source],
            dst_ref=recvbuf.at[g, slot, source],
            send_sem=send_sem.at[g, slot, d],
            recv_sem=recv_sem.at[g, slot, d],
            device_id=(source, mi),
            device_id_type=MESH,
        )

    order = sorted(range(1, n), key=lambda d: abs(2 * d - n))

    for copy in small:
        copy.wait()

    wide_vox = weight_pad.shape[1]
    halo_rows = n * block
    index_pad[...] = jnp.full_like(index_pad, -1)
    weight_pad[...] = jnp.zeros_like(weight_pad)
    index_pad[:, 0:vox] = index_ref[...]
    weight_pad[:, 0:vox] = weight_ref[...]
    index = index_pad[...]
    weight = weight_pad[...]
    beyond = index - vox
    slots = jnp.where(beyond < 0, -1 - halo_rows, (beyond // cap) * block + beyond % cap)
    halo_iota = lax.broadcasted_iota(jnp.int32, (halo_rows, wide_vox), 0)
    own_iota = lax.broadcasted_iota(jnp.int32, (wide_vox, wide_vox), 0)
    own_lane = lax.broadcasted_iota(jnp.int32, (wide_vox, wide_vox), 1)
    own = jnp.where(own_iota == own_lane, 1.0, 0.0)
    for k in range(index.shape[0]):
        own = own + jnp.where(own_iota == index[k : k + 1], weight[k : k + 1], 0.0)
    own = own.T[:vox, :vox].astype(BF16)
    for m in range(pseudo):
        matrix = jnp.zeros((halo_rows, wide_vox), F32)
        for k in range(index.shape[0]):
            target = slots[k : k + 1] + m * cap
            matrix = matrix + jnp.where(halo_iota == target, weight[k : k + 1], 0.0)
        conn_ref[m, :, 0:halo_rows] = matrix.T[:vox].astype(BF16)
        conn_ref[m, :, halo_rows : halo_rows + vox] = own

    mine = send_ref[me]
    local = jnp.zeros((n, cap), jnp.int32)
    for b in range(boundary_ref.shape[1]):
        local = local + jnp.where(mine == b, boundary_ref[0:1, b : b + 1], 0)
    spread = jnp.where(
        lax.broadcasted_iota(jnp.int32, (cap, halo_rows), 1) % cap
        == lax.broadcasted_iota(jnp.int32, (cap, halo_rows), 0),
        1.0,
        0.0,
    )
    spread = jnp.dot(
        local.astype(F32), spread, precision=HIGHEST, preferred_element_type=F32
    )
    mine_row = lax.broadcasted_iota(jnp.int32, (n, halo_rows), 1) // block
    spread = jnp.where(
        mine_row == lax.broadcasted_iota(jnp.int32, (n, halo_rows), 0), spread, 0.0
    )
    source_row = jnp.sum(spread, axis=0, keepdims=True)
    lane = lax.broadcasted_iota(jnp.int32, (wide_vox, halo_rows), 1)
    lane_member = (lane % block) // cap
    voxel = lax.broadcasted_iota(jnp.int32, (wide_vox, halo_rows), 0).astype(F32)
    chosen = jnp.where(voxel == source_row, 1.0, 0.0)
    for m in range(pseudo):
        matrix = jnp.where(lane_member == m, chosen, 0.0)
        sel_ref[:, m * vox : (m + 1) * vox] = matrix.T[:, :vox].astype(BF16)

    def make_rate(g):
        rows = pl.ds(g * group, group)
        rate[rows] = jnp.tanh(cur[rows]).astype(BF16)

    def pieces(g):
        for h in range(parts):
            for m in range(group):
                yield rate[g * group + m, :, h * part : (h + 1) * part]

    def send(g, slot):
        picked = jnp.dot(
            sel_ref[...], jnp.concatenate(list(pieces(g)), axis=0), preferred_element_type=F32
        )
        sendbuf[g, slot] = picked.astype(BF16).reshape(n, block, part)
        for d in order:
            halo_copy(g, slot, d).start()
        recvbuf[g, slot, me] = sendbuf[g, slot, me]

    def receive(g, slot):
        for d in order:
            halo_arrival(g, slot, d).wait_recv()
        for d in order:
            halo_copy(g, slot, d).wait_send()

    def update(g, slot, k):
        halo = recvbuf[g, slot].reshape(halo_rows, part)
        drives = [
            jnp.dot(
                conn_ref[i],
                jnp.concatenate([halo, own_rows], axis=0),
                preferred_element_type=F32,
            ).astype(BF16)
            for i, own_rows in enumerate(pieces(g))
        ]
        inputs = jnp.concatenate(
            [
                jnp.concatenate([drives[h * group + m] for h in range(parts)], axis=1)
                for m in range(group)
            ],
            axis=0,
        )
        mixed = jnp.dot(inputs, w_ref[...], preferred_element_type=F32)
        rows = pl.ds(g * group, group)
        mixed = mixed.reshape(group, vox, width)
        cur[rows] = 0.5 * (cur[rows] + mixed) + noise[k, rows].astype(F32)

    def ens_piece(dev, g, c):
        return ens.at[dev, g, :, pl.ds(c * chunk, chunk)]

    def ens_copy(dev, g, c, target, send_to, recv_to):
        return pltpu.make_async_remote_copy(
            src_ref=ens_piece(dev, g, c),
            dst_ref=ens_piece(dev, g, c),
            send_sem=send_to,
            recv_sem=recv_to,
            device_id=(me, target),
            device_id_type=MESH,
        )

    far = range(2, nm, 2)

    def own_copy(g, c, d):
        target = sib if d == 0 else mem_peer(d)
        return ens_copy(mi, g, c, target, ens_send.at[g, c, d // 2], ens_recv.at[g, c, d // 2])

    def own_arrival(g, c, d):
        source = sib if d == 0 else lax.rem(mi + nm - d, nm)
        return ens_copy(source, g, c, source, ens_send.at[g, c, d // 2], ens_recv.at[g, c, d // 2])

    def forward_copy(g, c, d):
        source = lax.rem(mi + nm - d, nm)
        return ens_copy(
            source, g, c, sib, fwd_send.at[g, c, d // 2], ens_recv.at[g, c, nm // 2 + d // 2]
        )

    def forward_arrival(g, c, d):
        source = lax.rem(sib + nm - d, nm)
        return ens_copy(
            source, g, c, sib, fwd_send.at[g, c, d // 2], ens_recv.at[g, c, nm // 2 + d // 2]
        )

    obs = observed_ref.shape[1]
    padded[...] = jnp.zeros_like(padded)
    padded[0:1, 0:obs] = value_ref[...]
    padded[1:2, :] = jnp.ones((1, padded.shape[1]), F32)
    padded[1:2, 0:obs] = var_ref[...]
    padded[2:3, 0:obs] = observed_ref[...].astype(F32) + 1.0
    padded[8 : 8 + members, 0:obs] = pert_ref[:, 0, :]
    lanes = padded.shape[1]
    vox_iota = lax.broadcasted_iota(jnp.int32, (vox, lanes), 0).astype(F32) + 1.0
    pick = jnp.where(vox_iota == padded[2:3, :], 1.0, 0.0)

    def finish(g):
        rows = pl.ds(g * group, group)
        ens[mi, g] = cur[rows].astype(BF16)
        for c in range(chunks):
            for d in far:
                own_copy(g, c, d).start()
        for c in range(chunks):
            own_copy(g, c, 0).start()
        for m in range(group):
            seen = jnp.sum(cur[g * group + m] * readout_ref[...], axis=1, keepdims=True)
            images[mi, g * group + m, :] = jnp.sum(pick * seen, axis=0)

    last = steps - 1
    flight = groups
    for g in range(flight):
        state_copy(g).wait()
        make_rate(g)
        if g == 0:
            pl.semaphore_wait(barrier, n - 1 + nm - 1)
        send(g, 0)
    for k in range(steps):
        noise_copy(k).wait()
    for first in range(0, groups, flight):

        def step(k, carry):
            slot = lax.rem(k, 2)
            for g in range(first, first + flight):
                receive(g, slot)
                update(g, slot, k)
                make_rate(g)
                send(g, 1 - slot)
            return carry

        lax.fori_loop(0, last, step, 0)
        for g in range(first, first + flight):
            receive(g, last % 2)
            update(g, last % 2, last)
            if g + flight < groups:
                state_copy(g + flight).wait()
                make_rate(g + flight)
                send(g + flight, 0)
            finish(g)

    def img_copy(d):
        return pltpu.make_async_remote_copy(
            src_ref=images.at[mi],
            dst_ref=images.at[mi],
            send_sem=img_send.at[d],
            recv_sem=img_recv.at[d],
            device_id=(me, mem_peer(d)),
            device_id_type=MESH,
        )

    def img_arrival(d):
        source = lax.rem(mi + nm - d, nm)
        return pltpu.make_async_remote_copy(
            src_ref=images.at[source],
            dst_ref=images.at[source],
            send_sem=img_send.at[d],
            recv_sem=img_recv.at[d],
            device_id=(me, source),
            device_id_type=MESH,
        )

    for d in range(1, nm):
        img_copy(d).start()
    for d in range(1, nm):
        img_arrival(d).wait_recv()

    total = nm * members
    var = padded[1:2, :]
    innov = padded[0:1, :] + jnp.sqrt(var) * padded[8 : 8 + members, :] - images[mi]
    image_all = images[...].reshape(total, lanes)
    anomaly = image_all - jnp.mean(image_all, axis=0, keepdims=True)
    scaled = anomaly / (var * (total - 1))
    nt = (((1,), (1,)), ((), ()))
    system = lax.dot_general(
        scaled,
        jnp.concatenate([anomaly, innov], axis=0),
        nt,
        precision=HIGHEST,
        preferred_element_type=F32,
    )
    row_id = lax.broadcasted_iota(jnp.int32, system.shape, 0)
    col_id = lax.broadcasted_iota(jnp.int32, system.shape, 1)
    system = system + jnp.where(row_id == col_id, 1.0, 0.0)
    column_rows = lax.broadcasted_iota(jnp.int32, (total, 1), 0)
    for j in range(total):
        row = system[j : j + 1, :] / system[j : j + 1, j : j + 1]
        column = system[:, j : j + 1] - jnp.where(column_rows == j, 1.0, 0.0)
        system = system - column * row
    mix = system[:, total : total + members]
    mix = mix - jnp.mean(mix, axis=0, keepdims=True)

    sub = 16
    e1 = jnp.where(
        lax.broadcasted_iota(jnp.int32, (members * sub, members), 0) // sub
        == lax.broadcasted_iota(jnp.int32, (members * sub, members), 1),
        1.0,
        0.0,
    )
    e2 = jnp.where(
        lax.broadcasted_iota(jnp.int32, (total, total * sub), 1) // sub
        == lax.broadcasted_iota(jnp.int32, (total, total * sub), 0),
        1.0,
        0.0,
    )
    wide = lax.dot_general(e1, mix, nt, precision=HIGHEST, preferred_element_type=F32)
    wide = jnp.dot(wide, e2, precision=HIGHEST, preferred_element_type=F32)
    same = lax.rem(lax.broadcasted_iota(jnp.int32, wide.shape, 0), sub) == lax.rem(
        lax.broadcasted_iota(jnp.int32, wide.shape, 1), sub
    )
    wide = jnp.where(same, wide, 0.0)
    high = wide.astype(BF16)
    low = (wide - high.astype(F32)).astype(BF16)
    both = jnp.concatenate([high, low], axis=0)

    for g in range(groups - 1):
        for c in range(chunks):
            for d in far:
                own_arrival(g, c, d).wait_recv()
                forward_copy(g, c, d).start()
    for c in range(chunks):
        g = groups - 1
        for d in far:
            own_arrival(g, c, d).wait_recv()
            forward_copy(g, c, d).start()
        for g in range(groups):
            own_arrival(g, c, 0).wait_recv()
            for d in far:
                forward_arrival(g, c, d).wait_recv()
        for s in range(chunk // sub):
            rows = pl.ds(c * chunk + s * sub, sub)
            data = ens[:, :, :, rows].reshape(total * sub, width)
            added = jnp.dot(both, data, preferred_element_type=F32)
            half = members * sub
            added = (added[:half] + added[half:]).reshape(members, sub, width)
            cur[:, rows] = cur[:, rows] + added
        piece = pl.ds(c * chunk, chunk)
        pltpu.make_async_copy(cur.at[:, piece], out_hbm.at[:, piece], out_sem.at[c]).start()

    for c in range(chunks):
        piece = pl.ds(c * chunk, chunk)
        pltpu.make_async_copy(cur.at[:, piece], out_hbm.at[:, piece], out_sem.at[c]).wait()
        for g in range(groups):
            own_copy(g, c, 0).wait_send()
            for d in far:
                own_copy(g, c, d).wait_send()
                forward_copy(g, c, d).wait_send()
    for d in range(1, nm):
        img_copy(d).wait_send()


def per_device(
    state,
    noise,
    w_local,
    conn_weight,
    conn_index,
    boundary,
    send_pos,
    readout,
    observed,
    obs_value,
    obs_var,
    obs_pert,
):
    members, vox, width = state.shape
    steps = noise.shape[0]
    n = lax.axis_size("dom")
    nm = lax.axis_size("member")
    cap = send_pos.shape[2]
    obs = observed.shape[1]
    parts = 2
    group = max(1, 16 // (cap * parts))
    groups = members // group
    block = group * parts * cap
    chunk = 32
    wide_vox = -(-vox // 128) * 128
    halo_rows = n * block

    hbm = pl.BlockSpec(memory_space=pltpu.HBM)
    small = (
        w_local,
        conn_weight,
        conn_index,
        boundary,
        send_pos,
        readout[None, :],
        observed,
        obs_value,
        obs_var,
        obs_pert,
    )
    dma = pltpu.SemaphoreType.DMA
    chunks = vox // chunk
    lanes = -(-obs // 128) * 128
    return pl.pallas_call(
        functools.partial(kernel, n, nm, group, cap, chunk, parts),
        out_shape=jax.ShapeDtypeStruct(state.shape, F32),
        in_specs=[hbm] * 12,
        out_specs=pl.BlockSpec(memory_space=pl.ANY),
        scratch_shapes=[pltpu.VMEM(x.shape, x.dtype) for x in small]
        + [
            pltpu.VMEM((conn_index.shape[0], wide_vox), F32),
            pltpu.VMEM((conn_index.shape[0], wide_vox), jnp.int32),
            pltpu.VMEM((group * parts, vox, halo_rows + vox), BF16),
            pltpu.VMEM((halo_rows, group * parts * vox), BF16),
            dma((len(small),)),
            pltpu.VMEM((members, vox, width), F32),
            pltpu.VMEM((steps, members, vox, width), BF16),
            pltpu.VMEM((members, vox, width), BF16),
            pltpu.VMEM((groups, 2, n, block, width // parts), BF16),
            pltpu.VMEM((groups, 2, n, block, width // parts), BF16),
            pltpu.VMEM((nm, groups, group, vox, width), BF16),
            pltpu.VMEM((nm, members, lanes), F32),
            pltpu.VMEM((8 + members, lanes), F32),
            dma((groups,)),
            dma((steps,)),
            dma((groups, 2, n)),
            dma((groups, 2, n)),
            dma((groups, chunks, nm)),
            dma((groups, chunks, nm)),
            dma((groups, chunks, nm)),
            dma((nm,)),
            dma((nm,)),
            dma((chunks,)),
        ],
        compiler_params=pltpu.CompilerParams(
            collective_id=0, has_side_effects=True, vmem_limit_bytes=62 * 1024 * 1024
        ),
    )(
        state,
        noise,
        *small,
    )


def solution(mesh):
    in_specs = (
        P("member", "dom", None),
        P(None, "member", "dom", None),
        P(),
        P(None, "dom"),
        P(None, "dom"),
        P("dom", None),
        P(),
        P(),
        P("dom", None),
        P("dom", None),
        P("dom", None),
        P("member", "dom", None),
    )
    return jax.shard_map(
        per_device,
        mesh=mesh,
        in_specs=in_specs,
        out_specs=P("member", "dom", None),
        check_vma=False,
    )
```
